32 devices in a mesh: fsdp: 16 (over z, x, core), seq: 2 (over y).
Axes of the slice: x: 2, y: 2, z: 4, core: 2. Of those that a mesh axis runs over, the one named last changes fastest.
Arguments:
- latents: bfloat16 [16, 1024, 1024], P('fsdp', 'seq'), may hold values from -6 to 6
- conditioning: bfloat16 [16, 1024], P('fsdp'), may hold values from -6 to 6
- mod_weight: bfloat16 [1024, 6144], P('fsdp'), may hold values from -0.1875 to 0.1875
- mod_bias: bfloat16 [6144], P('fsdp'), may hold values from -2 to 2
- qkv_weight: bfloat16 [1024, 3072], P('fsdp'), may hold values from -0.1875 to 0.1875
- query_bias: bfloat16 [1024], P('fsdp'), may hold values from -3 to 3
- value_bias: bfloat16 [1024], P('fsdp'), may hold values from -3 to 3
- out_weight: bfloat16 [1024, 1024], P('fsdp'), may hold values from -3 to 3
- out_bias: bfloat16 [1024], P('fsdp'), may hold values from -2 to 2
- up_weight: bfloat16 [1024, 4096], P('fsdp'), may hold values from -0.1875 to 0.1875
- up_bias: bfloat16 [4096], P('fsdp'), may hold values from -3 to 3
- down_weight: bfloat16 [4096, 1024], P('fsdp'), may hold values from -0.09375 to 0.09375
- down_bias: bfloat16 [1024], P('fsdp'), may hold values from -2 to 2
- cotangent: bfloat16 [16, 1024, 1024], P('fsdp', 'seq'), may hold values from -6 to 6
Outputs:
- block_output: bfloat16 [16, 1024, 1024], P('fsdp', 'seq')
- latents_grad: float32 [16, 1024, 1024], P('fsdp', 'seq')
- conditioning_grad: float32 [16, 1024], P('fsdp')
- mod_weight_grad: float32 [1024, 6144], P('fsdp')
- mod_bias_grad: float32 [6144], P('fsdp')
- qkv_weight_grad: float32 [1024, 3072], P('fsdp')
- query_bias_grad: float32 [1024], P('fsdp')
- value_bias_grad: float32 [1024], P('fsdp')
- out_weight_grad: float32 [1024, 1024], P('fsdp')
- out_bias_grad: float32 [1024], P('fsdp')
- up_weight_grad: float32 [1024, 4096], P('fsdp')
- up_bias_grad: float32 [4096], P('fsdp')
- down_weight_grad: float32 [4096, 1024], P('fsdp')
- down_bias_grad: float32 [1024], P('fsdp')
The draws below stay inside these ranges and needn't reach their ends.
All inputs are finite; a program needn't handle non-finite values.
Results may differ from the reference program's by a relative error of at most 0.01.
The reference program's roundings to bfloat16 on the way count: a program that leaves them out, or rounds other values in their place, can miss the bound.
Values may be sent and summed in bfloat16 or wider, within the bound.
A program may use at most 192 MiB of HBM per device.

```python
import math
import jax
import jax.numpy as jnp
from jax import lax

D = 1024
H = 16
FF = 4096
LEN = 1024
HD = 64
LATENTS = 16


def levels(rng, extent, cuts, least, top_value):
    def one(axis_at, blocks):
        steps = jax.random.uniform(jax.random.fold_in(jax.random.fold_in(rng, 6), axis_at), (blocks,), jnp.float32, least / len(cuts), top_value / len(cuts))
        return jnp.repeat(jnp.exp(steps), extent[axis_at] // blocks).reshape((-1,) + (1,) * (len(extent) - axis_at - 1))

    factor_of = one(*cuts[0])
    for cut in cuts[1:]:
        factor_of = factor_of * one(*cut)
    return factor_of


def bell_draw(key, extent, deviation, most, shards=(), kind=jnp.bfloat16):
    array = deviation * jax.random.normal(key, extent, jnp.float32)
    if shards:
        array = array * levels(key, extent, shards, -0.22, 0.18)
    return jnp.clip(array, -most, most).astype(kind)


def setup_inputs(seed: int = 0) -> dict:
    seeds = jax.random.split(jax.random.key(seed), 15)
    latents = bell_draw(seeds[0], (LATENTS, LEN, D), 1.0, 6.0, ((0, 16), (1, 2)))
    conditioning = bell_draw(seeds[1], (LATENTS, D), 1.0, 6.0, ((0, 16),))
    mod_weight = bell_draw(seeds[2], (D, 6 * D), D ** -0.5, 0.1875, ((0, 16),))
    mod_bias = bell_draw(seeds[3], (6 * D,), 0.3, 2.0, ((0, 16),))
    qkv_weight = bell_draw(seeds[4], (D, 3 * D), D ** -0.5, 0.1875, ((0, 16),))
    query_bias = bell_draw(seeds[5], (D,), 0.5, 3.0, ((0, 16),))
    value_bias = bell_draw(seeds[6], (D,), 0.5, 3.0, ((0, 16),))
    out_weight = bell_draw(seeds[7], (D, D), (max(1, 4 * D // LEN)) ** -0.5, 3.0, ((0, 16),))
    out_bias = bell_draw(seeds[8], (D,), 0.3, 2.0, ((0, 16),))
    up_weight = bell_draw(seeds[9], (D, FF), D ** -0.5, 0.1875, ((0, 16),))
    up_bias = bell_draw(seeds[10], (FF,), 0.5, 3.0, ((0, 16),))
    down_weight = bell_draw(seeds[11], (FF, D), FF ** -0.5, 0.09375, ((0, 16),))
    down_bias = bell_draw(seeds[12], (D,), 0.3, 2.0, ((0, 16),))
    cotangent = bell_draw(seeds[13], (LATENTS, LEN, D), 1.0, 6.0, ((0, 16), (1, 2)))
    return dict(latents=latents, conditioning=conditioning, mod_weight=mod_weight, mod_bias=mod_bias, qkv_weight=qkv_weight, query_bias=query_bias, value_bias=value_bias, out_weight=out_weight, out_bias=out_bias, up_weight=up_weight, up_bias=up_bias, down_weight=down_weight, down_bias=down_bias, cotangent=cotangent)


@jax.custom_vjp
def low(v):
    return lax.optimization_barrier(v.astype(jnp.bfloat16)).astype(jnp.float32)

@jax.custom_vjp
def low_back(v):
    return v

def low_keep(v):
    return (low(v), None)

def low_pass(kept, grad):
    return (grad,)

def back_keep(v):
    return (v, None)

def back_low(kept, grad):
    return (low(grad),)
low.defvjp(low_keep, low_pass)
low_back.defvjp(back_keep, back_low)
EPSILON = 1e-06
HIGHEST = lax.Precision.HIGHEST

def norm_rows(values):
    centred = values - lax.optimization_barrier(jnp.mean(values, axis=-1, keepdims=True))
    return centred * lax.rsqrt(lax.optimization_barrier(jnp.mean(centred * centred, axis=-1, keepdims=True)) + EPSILON)

def attend_block(query_block, keys, values):
    factor = 1.0 / math.sqrt(query_block.shape[-1])
    scores = low_back(jnp.einsum('qhd,khd->hqk', query_block, keys, precision=HIGHEST) * factor)
    probs = jax.nn.softmax(scores, axis=-1)
    mixed = jnp.einsum('hqk,khd->qhd', low(probs), values, precision=HIGHEST)
    return mixed.reshape(query_block.shape[0], -1)

def one_latent(tokens, condition, mod_weight, mod_bias, qkv_weight, query_bias, value_bias, out_weight, out_bias, up_weight, up_bias, down_weight, down_bias):
    length, width = tokens.shape
    modulation = low_back(jnp.dot(low(jax.nn.silu(condition)), mod_weight, precision=HIGHEST) + mod_bias)
    modulation = modulation.reshape(6, width)
    attn_input = low(norm_rows(tokens) * (1.0 + modulation[1]) + modulation[0])
    bias_all = jnp.concatenate([query_bias, jnp.zeros_like(query_bias), value_bias])
    projected = low(low_back(jnp.dot(attn_input, qkv_weight, precision=HIGHEST) + bias_all))
    projected = projected.reshape(length, 3, H, HD)
    keys = projected[:, 1]
    values = projected[:, 2]
    block = min(512, length)
    query_blocks = projected[:, 0].reshape(length // block, block, H, HD)

    def per_block(query_block):
        return attend_block(query_block, keys, values)
    mixed = lax.map(jax.checkpoint(per_block), query_blocks).reshape(length, width)
    attn_heads = low(low_back(mixed))
    attn_out = low_back(jnp.dot(attn_heads, out_weight, precision=HIGHEST) + out_bias)
    after_attn = tokens + modulation[2] * attn_out
    mlp_input = low(norm_rows(after_attn) * (1.0 + modulation[4]) + modulation[3])
    hidden_pre = low_back(jnp.dot(mlp_input, up_weight, precision=HIGHEST) + up_bias)
    hidden_act = low(jax.nn.gelu(hidden_pre, approximate=True))
    branch_out = low_back(jnp.dot(hidden_act, down_weight, precision=HIGHEST) + down_bias)
    return after_attn + modulation[5] * branch_out

def reference(latents, conditioning, mod_weight, mod_bias, qkv_weight, query_bias, value_bias, out_weight, out_bias, up_weight, up_bias, down_weight, down_bias, cotangent):
    arrays = tuple((item.astype(jnp.float32) for item in (latents, conditioning, mod_weight, mod_bias, qkv_weight, query_bias, value_bias, out_weight, out_bias, up_weight, up_bias, down_weight, down_bias)))

    def forward(inputs, conds, *weights):

        def per_latent(pair):
            return one_latent(pair[0], pair[1], *weights)
        return lax.map(per_latent, (inputs, conds))
    result, pullback = jax.vjp(forward, *arrays)
    grads = pullback(cotangent.astype(jnp.float32))
    return (result.astype(jnp.bfloat16), grads[0], grads[1], grads[2], grads[3], grads[4], grads[5], grads[6], grads[7], grads[8], grads[9], grads[10], grads[11], grads[12])
```

```python
import functools

import jax
import jax.numpy as jnp
from jax import lax
from jax.experimental import pallas as pl
from jax.experimental.pallas import tpu as pltpu
from jax.sharding import PartitionSpec as P

HD = 64


EPSILON = 1e-06


def norm_rows(values):
    centred = values - jnp.mean(values, axis=-1, keepdims=True)
    inverse = lax.rsqrt(jnp.mean(centred * centred, axis=-1, keepdims=True) + EPSILON)
    return (centred * inverse, inverse)


def norm_back(grad_normed, normed, inverse):
    mean_grad = jnp.mean(grad_normed, axis=-1, keepdims=True)
    mean_cross = jnp.mean(grad_normed * normed, axis=-1, keepdims=True)
    return inverse * (grad_normed - mean_grad - normed * mean_cross)


def project(left, weight):
    return lax.dot_general(
        left, weight, (((left.ndim - 1,), (0,)), ((), ())), preferred_element_type=jnp.float32
    )


def project_back(left, weight):
    return lax.dot_general(
        left, weight, (((left.ndim - 1,), (1,)), ((), ())), preferred_element_type=jnp.float32
    )


def weight_term(inputs, grads):
    return lax.dot_general(
        inputs, grads, (((0,), (0,)), ((), ())), preferred_element_type=jnp.float32
    )


def nt(left, right):
    return lax.dot_general(
        left, right, (((1,), (1,)), ((), ())), preferred_element_type=jnp.float32
    )


def nn(left, right):
    return jnp.dot(left, right, preferred_element_type=jnp.float32)


def forward_kernel(query_ref, key_ref, value_ref, out_ref, *, block):
    length, lanes = query_ref.shape
    factor = HD**-0.5
    for head in range(lanes // HD):
        cols = slice(head * HD, (head + 1) * HD)
        keys = key_ref[:, cols]
        values = value_ref[:, cols]

        def one_block(at, carry):
            rows = pl.ds(pl.multiple_of(at * block, block), block)
            scores = nt(query_ref[rows, cols] * factor, keys)
            exponent = jnp.exp(scores - jnp.max(scores, axis=-1, keepdims=True))
            totals = jnp.sum(exponent, axis=-1, keepdims=True)
            probs = (exponent * (1.0 / totals)).astype(jnp.bfloat16)
            out_ref[rows, cols] = nn(probs, values).astype(jnp.bfloat16)
            return carry

        lax.fori_loop(0, length // block, one_block, 0)


def backward_kernel(
    query_ref, key_ref, value_ref, grad_ref, query_grad, key_grad, value_grad, *, block
):
    length, lanes = query_ref.shape
    factor = HD**-0.5
    for head in range(lanes // HD):
        cols = slice(head * HD, (head + 1) * HD)
        keys = key_ref[:, cols]
        values = value_ref[:, cols]
        keys_turned = (keys * factor).T

        def one_block(at, carry):
            key_sum, value_sum = carry
            rows = pl.ds(pl.multiple_of(at * block, block), block)
            queries = query_ref[rows, cols] * factor
            grads = grad_ref[rows, cols]
            scores = nt(keys, queries)
            exponent = jnp.exp(scores - jnp.max(scores, axis=0, keepdims=True))
            probs = exponent * (1.0 / jnp.sum(exponent, axis=0, keepdims=True))
            grad_probs = nt(values, grads)
            cross = probs * grad_probs
            inner = jnp.sum(cross, axis=0, keepdims=True)
            grad_scores = (cross - probs * inner).astype(jnp.bfloat16)
            value_sum = value_sum + nn(probs.astype(jnp.bfloat16), grads)
            key_sum = key_sum + nn(grad_scores, queries)
            query_grad[rows, cols] = nn(keys_turned, grad_scores).T.astype(jnp.bfloat16)
            return (key_sum, value_sum)

        zeros = jnp.zeros((length, HD), jnp.float32)
        key_sum, value_sum = lax.fori_loop(0, length // block, one_block, (zeros, zeros))
        key_grad[:, cols] = key_sum.astype(jnp.bfloat16)
        value_grad[:, cols] = value_sum.astype(jnp.bfloat16)


def attend(kernel, arrays, outs, block, dots):
    count, length = arrays[0][0].shape[:2]
    part = outs[0][2]
    lanes = min(128, part)

    def spec(first):
        return pl.BlockSpec((None, length, lanes), lambda b, h, first=first: (b, 0, first + h))

    result = pl.pallas_call(
        functools.partial(kernel, block=block),
        grid=(count, part // lanes),
        in_specs=[spec(first) for _, first in arrays],
        out_specs=[spec(0) for _ in outs],
        out_shape=[jax.ShapeDtypeStruct(out, jnp.bfloat16) for out in outs],
        cost_estimate=pl.CostEstimate(
            flops=8 * dots * count * length * length * part,
            bytes_accessed=2 * count * length * part * (len(arrays) + len(outs)),
            transcendentals=count * length * length * (part // HD),
        ),
        compiler_params=pltpu.CompilerParams(vmem_limit_bytes=48 * 1024 * 1024),
    )(*[array for array, _ in arrays])
    return result


class Tokens:
    def __init__(self, size):
        self.size = size
        self.me = lax.axis_index("seq")

    def swap(self, values):
        return lax.ppermute(values, "seq", [(0, 1), (1, 0)])

    def gather(self, values):
        if self.size == 2:
            return jnp.concatenate([values, self.swap(values)], axis=1)
        return lax.all_gather(values, "seq", axis=1, tiled=True)

    def own(self, values):
        local = values.shape[1] // self.size
        if self.size == 2:
            return values[:, :local]
        return lax.dynamic_slice_in_dim(values, self.me * local, local, 1)

    def scatter(self, left, product):
        local = left.shape[1] // self.size
        if self.size == 2:
            sent = self.swap(product(left[:, local:]).astype(jnp.bfloat16))
            return product(left[:, :local]) + sent.astype(jnp.float32)
        return lax.psum_scatter(
            product(left).astype(jnp.bfloat16), "seq", scatter_dimension=1, tiled=True
        ).astype(jnp.float32)

    def to_tokens(self, values):
        local = values.shape[1] // self.size
        if self.size == 2:
            own = values[:, :local]
            other = self.swap(values[:, local:])
            first = self.me == 0
            return jnp.concatenate(
                [jnp.where(first, own, other), jnp.where(first, other, own)], axis=2
            )
        return lax.all_to_all(values, "seq", split_axis=1, concat_axis=2, tiled=True)

    def to_heads(self, values):
        part = values.shape[2] // self.size
        if self.size == 2:
            first = self.me == 0
            low, high = values[:, :, :part], values[:, :, part:]
            other = self.swap(jnp.where(first, high, low))
            return jnp.concatenate([jnp.where(first, low, high), other], axis=1)
        return lax.all_to_all(values, "seq", split_axis=2, concat_axis=1, tiled=True)


def gather_rows(shard):
    return lax.all_gather(shard, "fsdp", axis=0, tiled=True)


def scatter_rows(term):
    return lax.psum_scatter(term.astype(jnp.bfloat16), "fsdp", scatter_dimension=0, tiled=True)


def gelu_parts(value):
    return jax.vjp(lambda v: jax.nn.gelu(v, approximate=True), value)


def per_device(
    fsdp,
    seq,
    latents,
    conditioning,
    mod_weight,
    mod_bias,
    qkv_weight,
    query_bias,
    value_bias,
    out_weight,
    out_bias,
    up_weight,
    up_bias,
    down_weight,
    down_bias,
    cotangent,
):
    f32 = jnp.float32
    count, local_len, width = latents.shape
    length = local_len * seq
    hidden = up_weight.shape[1]
    part = width // seq
    unit = hidden // (fsdp * seq)
    mine = lax.axis_index("seq")
    owner = lax.axis_index("fsdp")
    tokens = Tokens(seq)
    mod_rows = mod_weight.shape[0]

    cond_float = conditioning.astype(f32)
    silu_local = jax.nn.silu(cond_float).astype(jnp.bfloat16)
    small = jnp.concatenate(
        [silu_local.reshape(-1), query_bias, value_bias, out_bias, up_bias, down_bias]
    )
    small = lax.all_gather(small, "fsdp", axis=0)
    cuts = [count * width]
    for vector in (query_bias, value_bias, out_bias, up_bias, down_bias):
        cuts.append(cuts[-1] + vector.shape[0])
    silu_all = small[:, : cuts[0]].reshape(fsdp * count, width)
    full_query_bias, full_value_bias, full_out_bias, full_up_bias, full_down_bias = (
        small[:, start:stop].reshape(-1).astype(f32) for start, stop in zip(cuts, cuts[1:])
    )

    qkv_shard = lax.dynamic_slice_in_dim(
        qkv_weight.reshape(-1, 3, width), mine * part, part, 2
    ).reshape(-1, 3 * part)
    part_qkv = gather_rows(qkv_shard)
    full_out = gather_rows(out_weight)
    up_shard = lax.dynamic_index_in_dim(
        up_weight.reshape(-1, fsdp, seq, unit), mine, 2, keepdims=False
    ).reshape(-1, fsdp * unit)
    part_up = gather_rows(up_shard)
    part_down = gather_rows(lax.dynamic_slice_in_dim(down_weight, mine * unit, unit, 0))
    part_up_bias = lax.dynamic_index_in_dim(
        full_up_bias.reshape(fsdp, seq, unit), mine, 1, keepdims=False
    ).reshape(-1)

    silu_rows = lax.dynamic_slice_in_dim(silu_all, owner * mod_rows, mod_rows, 1)
    mod_term = project(silu_rows, mod_weight)
    columns = mod_bias.shape[0]
    placed = lax.dynamic_update_slice_in_dim(
        jnp.zeros((6 * width,), f32), mod_bias.astype(f32), owner * columns, 0
    )
    modulation = lax.psum_scatter(
        mod_term + placed, "fsdp", scatter_dimension=0, tiled=True
    ).reshape(count, 6, 1, width)
    shift_one = modulation[:, 0]
    scale_one = modulation[:, 1]
    gate_one = modulation[:, 2]
    shift_two = modulation[:, 3]
    scale_two = modulation[:, 4]
    gate_two = modulation[:, 5]

    all_latents = tokens.gather(latents)
    all_cotangent = tokens.gather(cotangent)
    normed_one, _ = norm_rows(all_latents.astype(f32))
    attn_input = (normed_one * (1.0 + scale_one) + shift_one).astype(jnp.bfloat16)
    bias_part = jnp.concatenate(
        [
            lax.dynamic_slice_in_dim(full_query_bias, mine * part, part, 0),
            jnp.zeros((part,), f32),
            lax.dynamic_slice_in_dim(full_value_bias, mine * part, part, 0),
        ]
    )
    by_heads = (project(attn_input, part_qkv) + bias_part).astype(jnp.bfloat16)
    groups = part // min(128, part)
    streams = [(by_heads, 0), (by_heads, groups), (by_heads, 2 * groups)]
    block = min(256, length)
    head_shape = (count, length, part)
    (mixed,) = attend(forward_kernel, streams, [head_shape], block, 2)
    attn_heads = tokens.to_tokens(mixed)
    inputs = latents.astype(f32)
    attn_out = project(attn_heads, full_out) + full_out_bias
    after_attn = inputs + gate_one * attn_out
    normed_two, inverse_two = norm_rows(after_attn)
    mlp_local = (normed_two * (1.0 + scale_two) + shift_two).astype(jnp.bfloat16)
    mlp_input = tokens.gather(mlp_local)
    hidden_pre = project(mlp_input, part_up) + part_up_bias
    grad_branch = (gate_two * all_cotangent.astype(f32)).astype(jnp.bfloat16)
    hidden_act, gelu_back = gelu_parts(hidden_pre)
    hidden_act = hidden_act.astype(jnp.bfloat16)
    grad_act = project_back(grad_branch, part_down)
    grad_pre = gelu_back(grad_act)[0].astype(jnp.bfloat16)
    grad_mlp_in = tokens.scatter(grad_pre, lambda rows: project_back(rows, part_up))

    rows = count * length
    flat_branch = grad_branch.reshape(rows, width)
    flat_pre = grad_pre.reshape(rows, -1)
    down_part = scatter_rows(weight_term(hidden_act.reshape(rows, -1), flat_branch))
    up_part = scatter_rows(weight_term(mlp_input.reshape(rows, width), flat_pre))
    up_bias_term = jnp.sum(flat_pre.astype(f32), axis=0)
    own_branch = tokens.own(grad_branch)
    down_bias_term = jnp.sum(own_branch.astype(f32), axis=(0, 1))

    branch_out = tokens.scatter(hidden_act, lambda rows: project(rows, part_down)) + full_down_bias
    block_output = (after_attn + gate_two * branch_out).astype(jnp.bfloat16)
    grad_out = cotangent.astype(f32)
    grad_gate_two = jnp.sum(grad_out * branch_out, axis=1)

    grad_scale_two = jnp.sum(grad_mlp_in * normed_two, axis=1)
    grad_shift_two = jnp.sum(grad_mlp_in, axis=1)
    grad_after = grad_out + norm_back(grad_mlp_in * (1.0 + scale_two), normed_two, inverse_two)
    grad_attn = (gate_one * grad_after).astype(jnp.bfloat16)
    grad_gate_one = jnp.sum(grad_after * attn_out, axis=1)
    grad_heads = project_back(grad_attn, full_out).astype(jnp.bfloat16)
    grad_mixed = tokens.to_heads(grad_heads)
    flat_attn = grad_attn.reshape(count * local_len, width)
    out_part = scatter_rows(weight_term(attn_heads.reshape(count * local_len, width), flat_attn))
    out_bias_term = jnp.sum(flat_attn.astype(f32), axis=0)

    grads = attend(
        backward_kernel, streams + [(grad_mixed, 0)], [head_shape] * 3, block, 5
    )
    grad_projected = jnp.concatenate(grads, axis=2)
    flat_projected = grad_projected.reshape(rows, 3 * part)
    qkv_part = scatter_rows(weight_term(attn_input.reshape(rows, width), flat_projected))
    column_sums = jnp.sum(flat_projected.astype(f32), axis=0)
    grad_attn_in = tokens.scatter(grad_projected, lambda rows: project_back(rows, part_qkv))
    own_normed, own_inverse = norm_rows(inputs)
    grad_scale_one = jnp.sum(grad_attn_in * own_normed, axis=1)
    grad_shift_one = jnp.sum(grad_attn_in, axis=1)
    latents_grad = grad_after + norm_back(
        grad_attn_in * (1.0 + scale_one), own_normed, own_inverse
    )

    early = jnp.concatenate(
        [
            jnp.concatenate(
                [grad_gate_one, grad_shift_two, grad_scale_two, grad_gate_two], axis=1
            ).reshape(-1),
            out_bias_term,
            down_bias_term,
            up_bias_term,
        ]
    )
    early = lax.all_gather(early, ("fsdp", "seq"), axis=0).reshape(fsdp, seq, -1)
    late = jnp.concatenate(
        [
            jnp.concatenate([grad_shift_one, grad_scale_one], axis=1).reshape(-1),
            column_sums[:part],
            column_sums[2 * part :],
        ]
    )
    late = lax.all_gather(late, ("fsdp", "seq"), axis=0).reshape(fsdp, seq, -1)
    at = count * 4 * width
    early_mod = jnp.sum(early[:, :, :at], axis=1).reshape(fsdp * count, 4 * width)
    early_bias = jnp.sum(early[:, :, at : at + 2 * width], axis=(0, 1))
    out_bias_total = lax.dynamic_slice_in_dim(
        early_bias[:width], owner * out_bias.shape[0], out_bias.shape[0], 0
    )
    down_bias_total = lax.dynamic_slice_in_dim(
        early_bias[width:], owner * down_bias.shape[0], down_bias.shape[0], 0
    )
    up_bias_all = early[:, :, at + 2 * width :].reshape(fsdp, seq, fsdp, unit)
    up_bias_total = jnp.sum(
        lax.dynamic_index_in_dim(up_bias_all, owner, 2, keepdims=False), axis=0
    ).reshape(-1)
    at = count * 2 * width
    late_mod = jnp.sum(late[:, :, :at], axis=1).reshape(fsdp * count, 2 * width)
    late_bias = jnp.sum(late[:, :, at:], axis=0).reshape(seq, 2, part)
    query_bias_total = lax.dynamic_slice_in_dim(
        late_bias[:, 0].reshape(-1), owner * query_bias.shape[0], query_bias.shape[0], 0
    )
    value_bias_total = lax.dynamic_slice_in_dim(
        late_bias[:, 1].reshape(-1), owner * value_bias.shape[0], value_bias.shape[0], 0
    )
    grad_modulation = jnp.concatenate([late_mod, early_mod], axis=1).astype(jnp.bfloat16)
    mod_total = weight_term(silu_rows, grad_modulation)
    mod_bias_total = jnp.sum(
        lax.dynamic_slice_in_dim(grad_modulation, owner * columns, columns, 1).astype(f32), axis=0
    )
    grad_silu_rows = project_back(grad_modulation, mod_weight)
    grad_silu_all = lax.all_gather(grad_silu_rows, "fsdp", axis=1, tiled=True)
    grad_silu = lax.dynamic_slice_in_dim(grad_silu_all, owner * count, count, 0)
    _, silu_back = jax.vjp(jax.nn.silu, cond_float)
    conditioning_grad = silu_back(grad_silu)[0]

    down_total = lax.all_gather(down_part, "seq", axis=0, tiled=True).astype(f32)
    up_total = (
        lax.all_gather(up_part.reshape(-1, fsdp, 1, unit), "seq", axis=2, tiled=True)
        .reshape(-1, hidden)
        .astype(f32)
    )
    qkv_total = (
        lax.all_gather(qkv_part.reshape(-1, 3, part), "seq", axis=2, tiled=True)
        .reshape(-1, 3 * width)
        .astype(f32)
    )
    out_total = lax.psum(out_part.astype(f32), "seq")
    return (
        block_output,
        latents_grad,
        conditioning_grad,
        mod_total,
        mod_bias_total,
        qkv_total,
        query_bias_total,
        value_bias_total,
        out_total,
        out_bias_total,
        up_total,
        up_bias_total,
        down_total,
        down_bias_total,
    )


def solution(mesh):
    return jax.shard_map(
        functools.partial(per_device, mesh.shape["fsdp"], mesh.shape["seq"]),
        mesh=mesh,
        in_specs=(
            P("fsdp", "seq", None),
            P("fsdp", None),
            P("fsdp", None),
            P("fsdp"),
            P("fsdp", None),
            P("fsdp"),
            P("fsdp"),
            P("fsdp", None),
            P("fsdp"),
            P("fsdp", None),
            P("fsdp"),
            P("fsdp", None),
            P("fsdp"),
            P("fsdp", "seq", None),
        ),
        out_specs=(
            P("fsdp", "seq", None),
            P("fsdp", "seq", None),
            P("fsdp", None),
            P("fsdp", None),
            P("fsdp"),
            P("fsdp", None),
            P("fsdp"),
            P("fsdp"),
            P("fsdp", None),
            P("fsdp"),
            P("fsdp", None),
            P("fsdp"),
            P("fsdp", None),
            P("fsdp"),
        ),
        check_vma=False,
    )
```

```python
import functools

import jax
import jax.numpy as jnp
from jax import lax
from jax.experimental import pallas as pl
from jax.experimental.pallas import tpu as pltpu
from jax.sharding import PartitionSpec as P

HD = 64


EPSILON = 1e-06


def norm_rows(values):
    centred = values - jnp.mean(values, axis=-1, keepdims=True)
    inverse = lax.rsqrt(jnp.mean(centred * centred, axis=-1, keepdims=True) + EPSILON)
    return (centred * inverse, inverse)


def norm_back(grad_normed, normed, inverse):
    mean_grad = jnp.mean(grad_normed, axis=-1, keepdims=True)
    mean_cross = jnp.mean(grad_normed * normed, axis=-1, keepdims=True)
    return inverse * (grad_normed - mean_grad - normed * mean_cross)


def project(left, weight):
    return lax.dot_general(
        left, weight, (((left.ndim - 1,), (0,)), ((), ())), preferred_element_type=jnp.float32
    )


def project_back(left, weight):
    return lax.dot_general(
        left, weight, (((left.ndim - 1,), (1,)), ((), ())), preferred_element_type=jnp.float32
    )


def weight_term(inputs, grads):
    return lax.dot_general(
        inputs, grads, (((0,), (0,)), ((), ())), preferred_element_type=jnp.float32
    )


def nt(left, right):
    return lax.dot_general(
        left, right, (((1,), (1,)), ((), ())), preferred_element_type=jnp.float32
    )


def nn(left, right):
    return jnp.dot(left, right, preferred_element_type=jnp.float32)


def forward_kernel(query_ref, key_ref, value_ref, out_ref, *, block):
    length, lanes = query_ref.shape
    factor = HD**-0.5
    for head in range(lanes // HD):
        cols = slice(head * HD, (head + 1) * HD)
        keys = key_ref[:, cols]
        values = value_ref[:, cols]

        def one_block(at, carry):
            rows = pl.ds(pl.multiple_of(at * block, block), block)
            scores = nt(query_ref[rows, cols] * factor, keys)
            exponent = jnp.exp(scores - jnp.max(scores, axis=-1, keepdims=True))
            totals = jnp.sum(exponent, axis=-1, keepdims=True)
            probs = (exponent * (1.0 / totals)).astype(jnp.bfloat16)
            out_ref[rows, cols] = nn(probs, values).astype(jnp.bfloat16)
            return carry

        lax.fori_loop(0, length // block, one_block, 0)


def backward_kernel(
    query_ref, key_ref, value_ref, grad_ref, query_grad, key_grad, value_grad, *, block
):
    length, lanes = query_ref.shape
    factor = HD**-0.5
    for head in range(lanes // HD):
        cols = slice(head * HD, (head + 1) * HD)
        keys = key_ref[:, cols]
        values = value_ref[:, cols]
        keys_turned = (keys * factor).T

        def one_block(at, carry):
            key_sum, value_sum = carry
            rows = pl.ds(pl.multiple_of(at * block, block), block)
            queries = query_ref[rows, cols] * factor
            grads = grad_ref[rows, cols]
            scores = nt(keys, queries)
            exponent = jnp.exp(scores - jnp.max(scores, axis=0, keepdims=True))
            probs = exponent * (1.0 / jnp.sum(exponent, axis=0, keepdims=True))
            grad_probs = nt(values, grads)
            cross = probs * grad_probs
            inner = jnp.sum(cross, axis=0, keepdims=True)
            grad_scores = (cross - probs * inner).astype(jnp.bfloat16)
            value_sum = value_sum + nn(probs.astype(jnp.bfloat16), grads)
            key_sum = key_sum + nn(grad_scores, queries)
            query_grad[rows, cols] = nn(keys_turned, grad_scores).T.astype(jnp.bfloat16)
            return (key_sum, value_sum)

        zeros = jnp.zeros((length, HD), jnp.float32)
        key_sum, value_sum = lax.fori_loop(0, length // block, one_block, (zeros, zeros))
        key_grad[:, cols] = key_sum.astype(jnp.bfloat16)
        value_grad[:, cols] = value_sum.astype(jnp.bfloat16)


def attend(kernel, arrays, outs, block, dots):
    count, length = arrays[0][0].shape[:2]
    part = outs[0][2]
    lanes = min(128, part)

    def spec(first):
        return pl.BlockSpec((None, length, lanes), lambda b, h, first=first: (b, 0, first + h))

    result = pl.pallas_call(
        functools.partial(kernel, block=block),
        grid=(count, part // lanes),
        in_specs=[spec(first) for _, first in arrays],
        out_specs=[spec(0) for _ in outs],
        out_shape=[jax.ShapeDtypeStruct(out, jnp.bfloat16) for out in outs],
        cost_estimate=pl.CostEstimate(
            flops=8 * dots * count * length * length * part,
            bytes_accessed=2 * count * length * part * (len(arrays) + len(outs)),
            transcendentals=count * length * length * (part // HD),
        ),
        compiler_params=pltpu.CompilerParams(vmem_limit_bytes=48 * 1024 * 1024),
    )(*[array for array, _ in arrays])
    return result


class Tokens:
    def __init__(self, size):
        self.size = size
        self.me = lax.axis_index("seq")

    def swap(self, values):
        return lax.ppermute(values, "seq", [(0, 1), (1, 0)])

    def gather(self, values):
        if self.size == 2:
            return jnp.concatenate([values, self.swap(values)], axis=1)
        return lax.all_gather(values, "seq", axis=1, tiled=True)

    def own(self, values):
        local = values.shape[1] // self.size
        if self.size == 2:
            return values[:, :local]
        return lax.dynamic_slice_in_dim(values, self.me * local, local, 1)

    def scatter(self, left, product):
        local = left.shape[1] // self.size
        if self.size == 2:
            sent = self.swap(product(left[:, local:]).astype(jnp.bfloat16))
            return product(left[:, :local]) + sent.astype(jnp.float32)
        return lax.psum_scatter(
            product(left).astype(jnp.bfloat16), "seq", scatter_dimension=1, tiled=True
        ).astype(jnp.float32)

    def to_tokens(self, values):
        local = values.shape[1] // self.size
        if self.size == 2:
            own = values[:, :local]
            other = self.swap(values[:, local:])
            first = self.me == 0
            return jnp.concatenate(
                [jnp.where(first, own, other), jnp.where(first, other, own)], axis=2
            )
        return lax.all_to_all(values, "seq", split_axis=1, concat_axis=2, tiled=True)

    def to_heads(self, values):
        part = values.shape[2] // self.size
        if self.size == 2:
            first = self.me == 0
            low, high = values[:, :, :part], values[:, :, part:]
            other = self.swap(jnp.where(first, high, low))
            return jnp.concatenate([jnp.where(first, low, high), other], axis=1)
        return lax.all_to_all(values, "seq", split_axis=2, concat_axis=1, tiled=True)


def gather_rows(shard):
    return lax.all_gather(shard, "fsdp", axis=0, tiled=True)


def scatter_rows(term):
    return lax.psum_scatter(term.astype(jnp.bfloat16), "fsdp", scatter_dimension=0, tiled=True)


def gelu_parts(value):
    return jax.vjp(lambda v: jax.nn.gelu(v, approximate=True), value)


def per_device(
    fsdp,
    seq,
    latents,
    conditioning,
    mod_weight,
    mod_bias,
    qkv_weight,
    query_bias,
    value_bias,
    out_weight,
    out_bias,
    up_weight,
    up_bias,
    down_weight,
    down_bias,
    cotangent,
):
    f32 = jnp.float32
    count, local_len, width = latents.shape
    length = local_len * seq
    hidden = up_weight.shape[1]
    part = width // seq
    unit = hidden // (fsdp * seq)
    mine = lax.axis_index("seq")
    owner = lax.axis_index("fsdp")
    tokens = Tokens(seq)
    mod_rows = mod_weight.shape[0]

    cond_float = conditioning.astype(f32)
    silu_local = jax.nn.silu(cond_float).astype(jnp.bfloat16)
    small = jnp.concatenate(
        [silu_local.reshape(-1), query_bias, value_bias, out_bias, up_bias, down_bias]
    )
    small = lax.all_gather(small, "fsdp", axis=0)
    cuts = [count * width]
    for vector in (query_bias, value_bias, out_bias, up_bias, down_bias):
        cuts.append(cuts[-1] + vector.shape[0])
    silu_all = small[:, : cuts[0]].reshape(fsdp * count, width)
    full_query_bias, full_value_bias, full_out_bias, full_up_bias, full_down_bias = (
        small[:, start:stop].reshape(-1).astype(f32) for start, stop in zip(cuts, cuts[1:])
    )

    qkv_shard = lax.dynamic_slice_in_dim(
        qkv_weight.reshape(-1, 3, width), mine * part, part, 2
    ).reshape(-1, 3 * part)
    part_qkv = gather_rows(qkv_shard)
    full_out = gather_rows(out_weight)
    up_shard = lax.dynamic_index_in_dim(
        up_weight.reshape(-1, fsdp, seq, unit), mine, 2, keepdims=False
    ).reshape(-1, fsdp * unit)
    part_up = gather_rows(up_shard)
    part_down = gather_rows(lax.dynamic_slice_in_dim(down_weight, mine * unit, unit, 0))
    part_up_bias = lax.dynamic_index_in_dim(
        full_up_bias.reshape(fsdp, seq, unit), mine, 1, keepdims=False
    ).reshape(-1)

    silu_rows = lax.dynamic_slice_in_dim(silu_all, owner * mod_rows, mod_rows, 1)
    mod_term = project(silu_rows, mod_weight)
    columns = mod_bias.shape[0]
    placed = lax.dynamic_update_slice_in_dim(
        jnp.zeros((6 * width,), f32), mod_bias.astype(f32), owner * columns, 0
    )
    terms = lax.all_to_all(mod_term + placed, "fsdp", split_axis=0, concat_axis=0, tiled=True)
    modulation = jnp.sum(terms.reshape(fsdp, count, 6, 1, width), axis=0)
    shift_one = modulation[:, 0]
    scale_one = modulation[:, 1]
    gate_one = modulation[:, 2]
    shift_two = modulation[:, 3]
    scale_two = modulation[:, 4]
    gate_two = modulation[:, 5]

    all_latents = tokens.gather(latents)
    all_cotangent = tokens.gather(cotangent)
    normed_one, _ = norm_rows(all_latents.astype(f32))
    attn_input = (normed_one * (1.0 + scale_one) + shift_one).astype(jnp.bfloat16)
    bias_part = jnp.concatenate(
        [
            lax.dynamic_slice_in_dim(full_query_bias, mine * part, part, 0),
            jnp.zeros((part,), f32),
            lax.dynamic_slice_in_dim(full_value_bias, mine * part, part, 0),
        ]
    )
    by_heads = (project(attn_input, part_qkv) + bias_part).astype(jnp.bfloat16)
    groups = part // min(128, part)
    streams = [(by_heads, 0), (by_heads, groups), (by_heads, 2 * groups)]
    block = min(256, length)
    head_shape = (count, length, part)
    (mixed,) = attend(forward_kernel, streams, [head_shape], block, 2)
    attn_heads = tokens.to_tokens(mixed)
    inputs = latents.astype(f32)
    attn_out = project(attn_heads, full_out) + full_out_bias
    after_attn = inputs + gate_one * attn_out
    normed_two, inverse_two = norm_rows(after_attn)
    mlp_local = (normed_two * (1.0 + scale_two) + shift_two).astype(jnp.bfloat16)
    mlp_input = tokens.gather(mlp_local)
    hidden_pre = project(mlp_input, part_up) + part_up_bias
    grad_branch = (gate_two * all_cotangent.astype(f32)).astype(jnp.bfloat16)
    hidden_act, gelu_back = gelu_parts(hidden_pre)
    hidden_act = hidden_act.astype(jnp.bfloat16)
    grad_act = project_back(grad_branch, part_down)
    grad_pre = gelu_back(grad_act)[0].astype(jnp.bfloat16)
    grad_mlp_in = tokens.scatter(grad_pre, lambda rows: project_back(rows, part_up))

    rows = count * length
    flat_branch = grad_branch.reshape(rows, width)
    flat_pre = grad_pre.reshape(rows, -1)
    down_term = weight_term(hidden_act.reshape(rows, -1), flat_branch).astype(jnp.bfloat16)
    up_term = weight_term(mlp_input.reshape(rows, width), flat_pre).astype(jnp.bfloat16)
    up_bias_term = jnp.sum(flat_pre.astype(f32), axis=0)
    own_branch = tokens.own(grad_branch)
    down_bias_term = jnp.sum(own_branch.astype(f32), axis=(0, 1))

    branch_out = tokens.scatter(hidden_act, lambda rows: project(rows, part_down)) + full_down_bias
    block_output = (after_attn + gate_two * branch_out).astype(jnp.bfloat16)
    grad_out = cotangent.astype(f32)
    grad_gate_two = jnp.sum(grad_out * branch_out, axis=1)

    grad_scale_two = jnp.sum(grad_mlp_in * normed_two, axis=1)
    grad_shift_two = jnp.sum(grad_mlp_in, axis=1)
    grad_after = grad_out + norm_back(grad_mlp_in * (1.0 + scale_two), normed_two, inverse_two)
    grad_attn = (gate_one * grad_after).astype(jnp.bfloat16)
    grad_gate_one = jnp.sum(grad_after * attn_out, axis=1)
    grad_heads = project_back(grad_attn, full_out).astype(jnp.bfloat16)
    grad_mixed, down_term, up_term = lax.optimization_barrier(
        (tokens.to_heads(grad_heads), down_term, up_term)
    )
    down_part = scatter_rows(down_term)
    up_part = scatter_rows(up_term)
    flat_attn = grad_attn.reshape(count * local_len, width)
    out_part = scatter_rows(weight_term(attn_heads.reshape(count * local_len, width), flat_attn))
    out_bias_term = jnp.sum(flat_attn.astype(f32), axis=0)

    grads = attend(
        backward_kernel, streams + [(grad_mixed, 0)], [head_shape] * 3, block, 5
    )
    grad_projected = jnp.concatenate(grads, axis=2)
    flat_projected = grad_projected.reshape(rows, 3 * part)
    qkv_part = scatter_rows(weight_term(attn_input.reshape(rows, width), flat_projected))
    column_sums = jnp.sum(flat_projected.astype(f32), axis=0)
    grad_attn_in = tokens.scatter(grad_projected, lambda rows: project_back(rows, part_qkv))
    own_normed, own_inverse = norm_rows(inputs)
    grad_scale_one = jnp.sum(grad_attn_in * own_normed, axis=1)
    grad_shift_one = jnp.sum(grad_attn_in, axis=1)
    latents_grad = grad_after + norm_back(
        grad_attn_in * (1.0 + scale_one), own_normed, own_inverse
    )

    early = jnp.concatenate(
        [
            jnp.concatenate(
                [grad_gate_one, grad_shift_two, grad_scale_two, grad_gate_two], axis=1
            ).reshape(-1),
            out_bias_term,
            down_bias_term,
            up_bias_term,
        ]
    )
    early_size = early.shape[0]
    late = jnp.concatenate(
        [
            jnp.concatenate([grad_shift_one, grad_scale_one], axis=1).reshape(-1),
            column_sums[:part],
            column_sums[2 * part :],
        ]
    )
    both = lax.all_gather(
        jnp.concatenate([early, late]), ("fsdp", "seq"), axis=0
    ).reshape(fsdp, seq, -1)
    early, late = both[:, :, :early_size], both[:, :, early_size:]
    at = count * 4 * width
    early_mod = jnp.sum(early[:, :, :at], axis=1).reshape(fsdp * count, 4 * width)
    early_bias = jnp.sum(early[:, :, at : at + 2 * width], axis=(0, 1))
    out_bias_total = lax.dynamic_slice_in_dim(
        early_bias[:width], owner * out_bias.shape[0], out_bias.shape[0], 0
    )
    down_bias_total = lax.dynamic_slice_in_dim(
        early_bias[width:], owner * down_bias.shape[0], down_bias.shape[0], 0
    )
    up_bias_all = early[:, :, at + 2 * width :].reshape(fsdp, seq, fsdp, unit)
    up_bias_total = jnp.sum(
        lax.dynamic_index_in_dim(up_bias_all, owner, 2, keepdims=False), axis=0
    ).reshape(-1)
    at = count * 2 * width
    late_mod = jnp.sum(late[:, :, :at], axis=1).reshape(fsdp * count, 2 * width)
    late_bias = jnp.sum(late[:, :, at:], axis=0).reshape(seq, 2, part)
    query_bias_total = lax.dynamic_slice_in_dim(
        late_bias[:, 0].reshape(-1), owner * query_bias.shape[0], query_bias.shape[0], 0
    )
    value_bias_total = lax.dynamic_slice_in_dim(
        late_bias[:, 1].reshape(-1), owner * value_bias.shape[0], value_bias.shape[0], 0
    )
    grad_modulation = jnp.concatenate([late_mod, early_mod], axis=1).astype(jnp.bfloat16)
    mod_total = weight_term(silu_rows, grad_modulation)
    mod_bias_total = jnp.sum(
        lax.dynamic_slice_in_dim(grad_modulation, owner * columns, columns, 1).astype(f32), axis=0
    )
    grad_silu_rows = project_back(grad_modulation, mod_weight)
    grad_silu_all = lax.all_gather(grad_silu_rows, "fsdp", axis=1, tiled=True)
    grad_silu = lax.dynamic_slice_in_dim(grad_silu_all, owner * count, count, 0)
    _, silu_back = jax.vjp(jax.nn.silu, cond_float)
    conditioning_grad = silu_back(grad_silu)[0]

    down_total = lax.all_gather(down_part, "seq", axis=0, tiled=True).astype(f32)
    up_total = (
        lax.all_gather(up_part.reshape(-1, fsdp, 1, unit), "seq", axis=2, tiled=True)
        .reshape(-1, hidden)
        .astype(f32)
    )
    qkv_total = (
        lax.all_gather(qkv_part.reshape(-1, 3, part), "seq", axis=2, tiled=True)
        .reshape(-1, 3 * width)
        .astype(f32)
    )
    out_total = lax.psum(out_part.astype(f32), "seq")
    return (
        block_output,
        latents_grad,
        conditioning_grad,
        mod_total,
        mod_bias_total,
        qkv_total,
        query_bias_total,
        value_bias_total,
        out_total,
        out_bias_total,
        up_total,
        up_bias_total,
        down_total,
        down_bias_total,
    )


def solution(mesh):
    return jax.shard_map(
        functools.partial(per_device, mesh.shape["fsdp"], mesh.shape["seq"]),
        mesh=mesh,
        in_specs=(
            P("fsdp", "seq", None),
            P("fsdp", None),
            P("fsdp", None),
            P("fsdp"),
            P("fsdp", None),
            P("fsdp"),
            P("fsdp"),
            P("fsdp", None),
            P("fsdp"),
            P("fsdp", None),
            P("fsdp"),
            P("fsdp", None),
            P("fsdp"),
            P("fsdp", "seq", None),
        ),
        out_specs=(
            P("fsdp", "seq", None),
            P("fsdp", "seq", None),
            P("fsdp", None),
            P("fsdp", None),
            P("fsdp"),
            P("fsdp", None),
            P("fsdp"),
            P("fsdp"),
            P("fsdp", None),
            P("fsdp"),
            P("fsdp", None),
            P("fsdp"),
            P("fsdp", None),
            P("fsdp"),
        ),
        check_vma=False,
    )
```
